32 devices in a mesh: dp: 4 (over z), tensor: 4 (over y, x), section: 2 (over core).
Axes of the slice: x: 2, y: 2, z: 4, core: 2. Of those that a mesh axis runs over, the one named last changes fastest.
Arguments:
- grad_kv: bfloat16 [512, 2, 2, 1024], P('dp', 'section', None, 'tensor'), may hold values from -6 to 6
- kv_weight: bfloat16 [2, 2, 1024, 8192], P('section', None, 'tensor'), may hold values from -0.0625 to 0.0625
- image_count: int32 [32], P('dp'), may hold values from 1 to 2
- tile_count: int32 [32, 2], P('dp'), may hold values from 1 to 4, as said below
- image_owner: int32 [32, 2], P('dp'), may hold values from 0 to 3, as said below
- proj_weight: bfloat16 [8192, 1280], P(('tensor', 'section')), may hold values from -0.15625 to 0.15625
- vision_states: bfloat16 [512, 1280], P('dp'), may hold values from -60 to 60
- norm_gain: float32 [1280], replicated, may hold values from 0.5 to 2
Outputs:
- grad_vision: float32 [512, 1280], P(('dp', 'tensor', 'section'))
The draws below stay inside these ranges and needn't reach their ends.
Inputs may be any that keep to these rules, and one draw needn't show every extreme that they name: `image_owner`: the 16 image slots of one decoder rank are shared evenly among the 4 owners, 4 slots each; live rows from one decoder rank to one owner number at most 32, and decoder rank 0 sends exactly 32 to owner 0. `tile_count`: some slots hold 4 tiles in every draw.
All inputs are finite; a program needn't handle non-finite values.
Results may differ from the reference program's by a relative error of at most 0.017.
Values may be sent and summed in bfloat16 or wider, within the bound.
A program may use at most 64 MiB of HBM per device.

```python
import math
import jax
import jax.numpy as jnp
from jax import lax

DM = 8192
VW = 1280
KVH = 8
HD = 128
IMG_MAX = 2
TILES = 4
TILE_TOK = 2
CROSS = 2
OWNERS = 4
HEAD_GROUP = 2
SLOTS = 16
ROWS_DEV = 128
SAMPLES = 32
TOKENS = 512
CAP = 32
OWN_ROWS = 128
DM_BLOCK = 1024
N_TENSOR = 4
N_SECTION = 2


def draw_tile_count(key, part):
    key = jax.random.fold_in(key, 11)
    tiles = jax.random.randint(key, (SAMPLES, IMG_MAX), 1, TILES + 1)
    slot_number = jnp.arange(SAMPLES * IMG_MAX).reshape(SAMPLES, IMG_MAX)
    forced = (slot_number < SLOTS) & (slot_number % OWNERS == 0)
    return jnp.where(forced, TILES, tiles).astype(jnp.int32)


def draw_image_owner(key, part):
    key = jax.random.fold_in(key, 23)
    scores = jax.random.randint(key, (OWNERS, OWNERS), 0, 1048576) * OWNERS + jnp.arange(OWNERS)[None, :]
    orders = jnp.argsort(scores, axis=1).astype(jnp.int32)
    orders = jnp.where(jnp.arange(OWNERS)[:, None] == 0, jnp.arange(OWNERS)[None, :], orders)
    slot_number = jnp.arange(SLOTS) % OWNERS
    owners_of = jnp.take(orders, slot_number, axis=1)
    return owners_of.reshape(SAMPLES, IMG_MAX).astype(jnp.int32)


def draw_vision_states(key, part):
    key = jax.random.fold_in(key, 37)
    first, second = jax.random.split(key, 2)
    count = OWNERS * OWN_ROWS
    scales = jnp.exp(jax.random.uniform(second, (count, 1), minval=0.0, maxval=math.log(10.0)))
    base = jax.random.normal(first, (count, VW))
    return (base * scales).astype(jnp.bfloat16)


def place_ends(entries, stream_key, low, high):
    longest = entries.shape.index(max(entries.shape))
    spots = []
    for shift in (0, 1):
        where = [jax.random.randint(jax.random.fold_in(stream_key, axis), (), 0, length) for axis, length in enumerate(entries.shape)]
        where[longest] = (where[longest] + shift) % entries.shape[longest]
        spots.append(tuple(where))
    return entries.at[spots[0]].set(low).at[spots[1]].set(high)


def steps_of(key, extent, cuts, least, top_value):
    loudness, own = 1.0, jax.random.fold_in(key, 6)
    for axis_at, parts in cuts:
        heights = jnp.exp(jax.random.uniform(jax.random.fold_in(own, axis_at), (parts,), jnp.float32, least / len(cuts), top_value / len(cuts)))
        loudness = loudness * jnp.repeat(heights, extent[axis_at] // parts).reshape([-1 if axis == axis_at else 1 for axis in range(len(extent))])
    return loudness


def centred(key, extent, scale, most, pieces=(), kind=jnp.bfloat16):
    array = jax.random.normal(key, extent, jnp.float32) * scale
    if len(pieces) > 0:
        array = steps_of(key, extent, pieces, -0.22, 0.18) * array
    return jnp.clip(array, min=-most, max=most).astype(kind)


def setup_inputs(seed: int = 0) -> dict:
    splits = jax.random.split(jax.random.key(seed), 9)
    return {
        "grad_kv": centred(splits[0], (TOKENS, CROSS, 2, KVH * HD), 1.0, 6.0, ((0, 4), (1, 2), (3, 4))),
        "kv_weight": centred(splits[1], (CROSS, 2, KVH * HD, DM), DM ** -0.5, 0.0625, ((0, 2), (2, 4))),
        "image_count": place_ends(jax.random.randint(splits[2], (SAMPLES,), 1, IMG_MAX + 1), jax.random.fold_in(splits[2], 1), 1, IMG_MAX).astype(jnp.int32),
        "tile_count": draw_tile_count(jax.random.fold_in(splits[8], 71), 0),
        "image_owner": draw_image_owner(jax.random.fold_in(splits[8], 71), 0),
        "proj_weight": centred(splits[5], (DM, VW), VW ** -0.5, 0.15625, ((0, 8),)),
        "vision_states": draw_vision_states(jax.random.fold_in(splits[8], 71), 0),
        "norm_gain": jnp.clip(jnp.exp(jax.random.uniform(splits[7], (VW,), jnp.float32, math.log(0.5), math.log(2.0))), 0.5, 2.0),
    }


def rounded_sum(total, product):
    return total + lax.optimization_barrier(product.astype(jnp.bfloat16)).astype(jnp.float32)

def reference(grad_kv, kv_weight, image_count, tile_count, image_owner, proj_weight, vision_states, norm_gain):
    head_cols = HEAD_GROUP * HD
    col_groups = N_TENSOR * N_SECTION
    img_rows = TILES * TILE_TOK

    def rank_grad(span_rows):
        total = jnp.zeros((ROWS_DEV, DM), jnp.float32)
        for layer in range(CROSS):
            for group in range(N_TENSOR):
                left_side = span_rows[:, layer, :, group * head_cols:(group + 1) * head_cols].reshape(ROWS_DEV, 2 * head_cols)
                right_side = kv_weight[layer, :, group * head_cols:(group + 1) * head_cols, :].reshape(2 * head_cols, DM)
                total = rounded_sum(total, jnp.dot(left_side, right_side, preferred_element_type=jnp.float32))
        return total.astype(jnp.bfloat16)
    feature_grad = lax.map(rank_grad, grad_kv.reshape(OWNERS, ROWS_DEV, CROSS, 2, KVH * HD)).reshape(TOKENS, DM)
    live_len = jnp.where(jnp.arange(IMG_MAX)[None, :] < image_count[:, None], tile_count * TILE_TOK, 0).reshape(OWNERS, SLOTS)
    dest_owner = image_owner.reshape(OWNERS, SLOTS)
    earlier = jnp.arange(SLOTS)[:, None] > jnp.arange(SLOTS)[None, :]
    same_owner = dest_owner[:, :, None] == dest_owner[:, None, :]
    offsets = lax.optimization_barrier(jnp.sum(jnp.where(same_owner & earlier[None], live_len[:, None, :], 0), axis=2))
    tok_index = jnp.arange(img_rows)
    targets = dest_owner[:, :, None] * OWN_ROWS + jnp.arange(OWNERS)[:, None, None] * CAP + offsets[:, :, None] + tok_index[None, None, :]
    targets = jnp.where(tok_index[None, None, :] < live_len[:, :, None], targets, OWNERS * OWN_ROWS).reshape(TOKENS)
    sources = jnp.full((OWNERS * OWN_ROWS + 1,), TOKENS, jnp.int32).at[targets].set(jnp.arange(TOKENS, dtype=jnp.int32))
    sources = sources[:OWNERS * OWN_ROWS].reshape(OWNERS, OWN_ROWS)
    padded_grad = jnp.concatenate([feature_grad, jnp.zeros((1, DM), jnp.bfloat16)], axis=0)

    def owner_grad(pair):
        source_rows, states = pair
        routed = padded_grad[source_rows]
        norm_grad = jnp.zeros((OWN_ROWS, VW), jnp.float32)
        for column in range(col_groups):
            product = jnp.dot(routed[:, column * DM_BLOCK:(column + 1) * DM_BLOCK], proj_weight[column * DM_BLOCK:(column + 1) * DM_BLOCK], preferred_element_type=jnp.float32)
            norm_grad = rounded_sum(norm_grad, product)
        inputs = states.astype(jnp.float32)
        centre = inputs - lax.optimization_barrier(jnp.mean(inputs, axis=1, keepdims=True))
        inverse = lax.rsqrt(lax.optimization_barrier(jnp.mean(centre * centre, axis=1, keepdims=True)) + 1e-05)
        normed = centre * inverse
        scaled = norm_grad * norm_gain
        return (scaled - lax.optimization_barrier(jnp.mean(scaled, axis=1, keepdims=True)) - normed * lax.optimization_barrier(jnp.mean(scaled * normed, axis=1, keepdims=True))) * inverse
    result = lax.map(owner_grad, (sources, vision_states.reshape(OWNERS, OWN_ROWS, VW)))
    return result.reshape(OWNERS * OWN_ROWS, VW)
```

```python
import functools
import jax
import jax.numpy as jnp
from jax import lax
from jax.experimental import pallas as pl
from jax.experimental.pallas import tpu as pltpu
from jax.sharding import PartitionSpec as P

TILE_TOK = 2
MESH = pl.DeviceIdType.MESH
F32 = jnp.float32
BF16 = jnp.bfloat16


def stage_of(q, bits):
    return bits - q.bit_length()


def block_mask(q, core, bits):
    mask = 0
    for step in range(bits):
        if q >> (bits - 1 - step) & 1:
            mask = mask + lax.shift_left(jnp.int32(1), jnp.int32((step + core) % bits))
    return mask


def xor(a, b, bits):
    total = 0
    for bit in range(bits):
        x, y = a // (1 << bit) % 2, b // (1 << bit) % 2
        total = total + (x + y - 2 * x * y) * (1 << bit)
    return total


def kernel(
    sizes, cnt_ref, til_ref, own_ref, grad_ref, w_hbm, proj_hbm, vis_hbm, gain_ref, out_ref,
    wbuf, pbuf, vbuf, sib_out, sib_in, local, half_out, half_in, term, pair_in, pair_out, chip_in,
    done, unit_in,
    w_sem, p_sem, v_sem, sib_s, sib_r, half_s, half_r, pair_s, pair_r, chip_s, chip_r, unit_s, unit_r,
):
    n_dp, n_t, bits, rows, cap, placed, share, unit, samples, slots = sizes
    groups = 2 * n_t
    dp, t, s = lax.axis_index("dp"), lax.axis_index("tensor"), lax.axis_index("section")
    g = t * 2 + s
    other = 1 - s
    col = wbuf.shape[2]
    units = share // unit
    early = placed <= rows

    def flip(t_index, step, core):
        bit = 1
        if bits > 1:
            shift = (step + core) % bits
            bit = sum(jnp.where(shift == i, 1 << i, 0) for i in range(bits))
        digit = t_index // bit % 2
        return t_index + (1 - 2 * digit) * bit

    def tensor_of(q, core):
        index = t
        for step in range(bits):
            if q >> (bits - 1 - step) & 1:
                index = flip(index, step, core)
        return index

    order = []
    for q in reversed(range(n_t)):
        order.append((q, True))
        if q < n_t - 1:
            order.append((q + 1, False))
    order.append((0, False))
    w_copies = {}
    for i, (q, sibling) in enumerate(order):
        core = other if sibling else s
        block = tensor_of(q, core) * 2 + core
        cp = pltpu.make_async_copy(
            w_hbm.at[:, pl.ds(pl.multiple_of(block * col, 128), col)], wbuf.at[i], w_sem.at[i]
        )
        cp.start()
        w_copies[q, sibling] = (i, cp)
    v_copy = pltpu.make_async_copy(vis_hbm.at[pl.ds(pl.multiple_of(g * share, 16), share)], vbuf, v_sem)
    v_copy.start()
    p_copy = pltpu.make_async_copy(proj_hbm, pbuf, p_sem)
    p_copy.start()

    dests, sources = [], []
    for k in range(units):
        row = g * share + k * unit
        to = row // cap
        at = dp * cap + row % cap
        dests.append((to, at // share, at % share // unit))
        src_dp = row // cap
        src_row = dp * cap + row % cap
        sources.append((src_dp, src_row // share))

    def is_me(d_index, g_index):
        return jnp.logical_and(d_index == dp, g_index == g)

    barrier = pltpu.get_barrier_semaphore()
    pl.semaphore_signal(barrier, inc=1, device_id=(dp, t, other), device_id_type=MESH)
    for m in range(1, n_t):
        pl.semaphore_signal(barrier, inc=1, device_id=(dp, xor(t, m, bits), s), device_id_type=MESH)
    expect = jnp.int32(n_t)
    for k in range(units):
        src_dp, src_g = sources[k]

        @pl.when(jnp.logical_not(is_me(src_dp, src_g)))
        def _():
            pl.semaphore_signal(barrier, inc=1, device_id=(src_dp, src_g // 2, src_g % 2), device_id_type=MESH)

        expect = expect + jnp.where(is_me(dests[k][0], dests[k][1]), 0, 1)

    img_rows = rows // slots
    per = slots // samples
    live, owner = [], []
    for j in range(slots):
        live.append(jnp.where(j % per < cnt_ref[j // per], til_ref[j // per, j % per] * TILE_TOK, 0))
        owner.append(own_ref[j // per, j % per])
    lane = lax.broadcasted_iota(jnp.int32, (1, rows), 1)
    slot, tok = lane // img_rows, lane % img_rows
    target = jnp.full((1, rows), -1, jnp.int32)
    for j in range(slots):
        base = owner[j] * cap
        for i in range(j):
            base = base + jnp.where(owner[i] == owner[j], live[i], 0)
        target = jnp.where(slot == j, jnp.where(tok < live[j], base + tok, -1), target)
    placing = (lax.broadcasted_iota(jnp.int32, (placed, rows), 0) == target).astype(F32).astype(BF16)

    left = jnp.concatenate([grad_ref[:, 0, :], grad_ref[:, 1, :]], axis=1)
    if early:
        left = jnp.dot(placing, left, preferred_element_type=F32).astype(BF16)

    def multiply(q, sibling):
        i, cp = w_copies[q, sibling]
        cp.wait()
        return jnp.dot(left, wbuf[i], preferred_element_type=F32)

    def sib_copy(q):
        return pltpu.make_async_remote_copy(
            sib_out.at[q], sib_in.at[q], sib_s.at[q], sib_r.at[q], device_id=(dp, t, other), device_id_type=MESH
        )

    def half_copy(q):
        to = flip(t, stage_of(q, bits), s)
        return pltpu.make_async_remote_copy(
            half_out.at[q], half_in.at[q], half_s.at[q], half_r.at[q], device_id=(dp, to, s), device_id_type=MESH
        )

    first = True
    for q, sibling in order:
        if sibling:
            sib_out[q] = multiply(q, True).astype(BF16)
            if first:
                pl.semaphore_wait(barrier, expect)
                first = False
            sib_copy(q).start()
        else:
            value = multiply(q, False)
            sib_copy(q).wait_recv()
            value = value + sib_in[q].astype(F32)
            if q > 0 and stage_of(q, bits) == 0:
                half_out[q] = value.astype(BF16)
                half_copy(q).start()
            else:
                local[q] = value

    v_copy.wait()
    states = vbuf[...].astype(F32)
    centre = states - jnp.mean(states, axis=1, keepdims=True)
    inverse = lax.rsqrt(jnp.mean(centre * centre, axis=1, keepdims=True) + 1e-05)
    normed = centre * inverse

    for q in reversed(range(n_t // 2)):
        value = local[q]
        for step in range(stage_of(q, bits)):
            sent = q + (n_t >> (step + 1))
            half_copy(sent).wait_recv()
            value = value + half_in[sent].astype(F32)
        if q > 0:
            half_out[q] = value.astype(BF16)
            half_copy(q).start()
    features = value.astype(BF16)
    if not early:
        features = jnp.dot(placing, features, preferred_element_type=F32).astype(BF16)
    p_copy.wait()
    product = jnp.dot(features, pbuf[...], preferred_element_type=F32).astype(BF16)
    for i in range(groups):
        term[i % 2, i // 2] = product[i * share:(i + 1) * share]

    pair = pltpu.make_async_remote_copy(
        term.at[other], pair_in, pair_s, pair_r, device_id=(dp, t, other), device_id_type=MESH
    )
    pair.start()
    pair.wait_recv()

    def chip_copy(m):
        return pltpu.make_async_remote_copy(
            pair_out.at[m], chip_in.at[m], chip_s.at[m], chip_r.at[m],
            device_id=(dp, xor(t, m, bits), s), device_id_type=MESH,
        )

    for m in range(1, n_t):
        to = xor(t, m, bits)
        pair_out[m] = (term[s, to].astype(F32) + pair_in[to].astype(F32)).astype(BF16)
        chip_copy(m).start()
    total = term[s, t].astype(F32) + pair_in[t].astype(F32)
    for m in range(1, n_t):
        chip_copy(m).wait_recv()
        total = total + chip_in[m].astype(F32)
    for k in range(units):
        done[k] = total[k * unit:(k + 1) * unit].astype(done.dtype)

    def unit_copy(k):
        to, to_g, at = dests[k]
        return pltpu.make_async_remote_copy(
            done.at[k], unit_in.at[at], unit_s.at[k], unit_r.at[at],
            device_id=(to, to_g // 2, to_g % 2), device_id_type=MESH,
        )

    for k in range(units):
        mine = is_me(dests[k][0], dests[k][1])

        @pl.when(mine)
        def _():
            unit_in[dests[k][2]] = done[k]

        @pl.when(jnp.logical_not(mine))
        def _():
            unit_copy(k).start()

    for k in range(units):

        @pl.when(jnp.logical_not(is_me(*sources[k])))
        def _():
            pltpu.make_async_remote_copy(
                done.at[k], unit_in.at[k], unit_s.at[k], unit_r.at[k],
                device_id=(sources[k][0], sources[k][1] // 2, sources[k][1] % 2), device_id_type=MESH,
            ).wait_recv()

    norm_grad = jnp.concatenate([unit_in[k] for k in range(units)], axis=0).astype(F32)
    scaled = norm_grad * gain_ref[...]
    out_ref[...] = (
        scaled
        - jnp.mean(scaled, axis=1, keepdims=True)
        - normed * jnp.mean(scaled * normed, axis=1, keepdims=True)
    ) * inverse

    for q in range(n_t):
        sib_copy(q).wait_send()
    for q in range(1, n_t):
        half_copy(q).wait_send()
    pair.wait_send()
    for m in range(1, n_t):
        chip_copy(m).wait_send()
    for k in range(units):

        @pl.when(jnp.logical_not(is_me(dests[k][0], dests[k][1])))
        def _():
            unit_copy(k).wait_send()


def solution(mesh):
    n_dp, n_t = mesh.shape["dp"], mesh.shape["tensor"]
    bits = n_t.bit_length() - 1

    def per_device(grad_kv, kv_weight, image_count, tile_count, image_owner, proj_weight, vision_states, norm_gain):
        rows, width = grad_kv.shape[0], proj_weight.shape[1]
        depth = 2 * grad_kv.shape[3]
        samples = image_owner.shape[0]
        slots = samples * image_owner.shape[1]
        cap = rows // slots * max(1, slots // n_dp)
        placed = n_dp * cap
        share = placed // (2 * n_t)
        unit = min(cap, share)
        units = share // unit
        dm = kv_weight.shape[3]
        col = dm // (2 * n_t)
        mid = rows
        sizes = (n_dp, n_t, bits, rows, cap, placed, share, unit, samples, slots)
        moved = BF16 if unit % 16 == 0 else F32
        vmem, smem, hbm = (pl.BlockSpec(memory_space=m) for m in (pltpu.VMEM, pltpu.SMEM, pl.ANY))
        dma = pltpu.SemaphoreType.DMA
        return pl.pallas_call(
            functools.partial(kernel, sizes),
            out_shape=jax.ShapeDtypeStruct((share, width), F32),
            in_specs=[smem, smem, smem, vmem, hbm, hbm, hbm, vmem],
            out_specs=vmem,
            scratch_shapes=[
                pltpu.VMEM((2 * n_t, depth, col), BF16),
                pltpu.VMEM((col, width), BF16),
                pltpu.VMEM((share, width), BF16),
                pltpu.VMEM((n_t, mid, col), BF16),
                pltpu.VMEM((n_t, mid, col), BF16),
                pltpu.VMEM((max(1, n_t // 2), mid, col), F32),
                pltpu.VMEM((n_t, mid, col), BF16),
                pltpu.VMEM((n_t, mid, col), BF16),
                pltpu.VMEM((2, n_t, share, width), BF16),
                pltpu.VMEM((n_t, share, width), BF16),
                pltpu.VMEM((n_t, share, width), BF16),
                pltpu.VMEM((n_t, share, width), BF16),
                pltpu.VMEM((units, unit, width), moved),
                pltpu.VMEM((units, unit, width), moved),
                dma((2 * n_t,)), dma, dma,
                dma((n_t,)), dma((n_t,)), dma((n_t,)), dma((n_t,)), dma, dma,
                dma((n_t,)), dma((n_t,)), dma((units,)), dma((units,)),
            ],
            compiler_params=pltpu.CompilerParams(
                collective_id=0, has_side_effects=True, vmem_limit_bytes=40 * 1024 * 1024
            ),
        )(
            image_count, tile_count, image_owner, grad_kv.reshape(rows, 2, grad_kv.shape[3]),
            kv_weight.reshape(depth, dm), proj_weight, vision_states, norm_gain.reshape(1, width),
        )

    return jax.shard_map(
        per_device,
        mesh=mesh,
        in_specs=(
            P("dp", "section", None, "tensor"),
            P("section", None, "tensor", None),
            P("dp"),
            P("dp", None),
            P("dp", None),
            P(("tensor", "section"), None),
            P("dp", None),
            P(),
        ),
        out_specs=P(("dp", "tensor", "section"), None),
        check_vma=False,
    )
```

```python
import functools
import jax
import jax.numpy as jnp
from jax import lax
from jax.experimental import pallas as pl
from jax.experimental.pallas import tpu as pltpu
from jax.sharding import PartitionSpec as P

TILE_TOK = 2
MESH = pl.DeviceIdType.MESH
F32 = jnp.float32
BF16 = jnp.bfloat16


def stage_of(q, bits):
    return bits - q.bit_length()


def block_mask(q, core, bits):
    mask = 0
    for step in range(bits):
        if q >> (bits - 1 - step) & 1:
            mask = mask + lax.shift_left(jnp.int32(1), jnp.int32((step + core) % bits))
    return mask


def xor(a, b, bits):
    total = 0
    for bit in range(bits):
        x, y = a // (1 << bit) % 2, b // (1 << bit) % 2
        total = total + (x + y - 2 * x * y) * (1 << bit)
    return total


def kernel(
    sizes, cnt_ref, til_ref, own_ref, grad_hbm, w_hbm, proj_hbm, vis_hbm, gain_hbm, out_ref,
    grad_ref, gain_ref,    wbuf, pbuf, vbuf, sib_out, sib_in, local, half_out, half_in, term, pair_in, pair_out, chip_in,
    done, unit_in,
    g_sem, n_sem, w_sem, p_sem, v_sem, sib_s, sib_r, half_s, half_r, pair_s, pair_r, chip_s, chip_r, unit_s, unit_r,
):
    n_dp, n_t, bits, rows, cap, placed, share, unit, samples, slots = sizes
    groups = 2 * n_t
    dp, t, s = lax.axis_index("dp"), lax.axis_index("tensor"), lax.axis_index("section")
    g = t * 2 + s
    other = 1 - s
    col = wbuf.shape[2]
    units = share // unit
    early = placed <= rows

    def flip(t_index, step, core):
        bit = 1
        if bits > 1:
            shift = (step + core) % bits
            bit = sum(jnp.where(shift == i, 1 << i, 0) for i in range(bits))
        digit = t_index // bit % 2
        return t_index + (1 - 2 * digit) * bit

    def tensor_of(q, core):
        index = t
        for step in range(bits):
            if q >> (bits - 1 - step) & 1:
                index = flip(index, step, core)
        return index

    order = []
    for q in reversed(range(n_t)):
        order.append((q, True))
        if q < n_t - 1:
            order.append((q + 1, False))
    order.append((0, False))
    g_copy = pltpu.make_async_copy(grad_hbm, grad_ref, g_sem)
    g_copy.start()
    w_copies = {}
    for i, (q, sibling) in enumerate(order):
        core = other if sibling else s
        block = tensor_of(q, core) * 2 + core
        cp = pltpu.make_async_copy(
            w_hbm.at[:, pl.ds(pl.multiple_of(block * col, 128), col)], wbuf.at[i], w_sem.at[i]
        )
        cp.start()
        w_copies[q, sibling] = (i, cp)
    v_copy = pltpu.make_async_copy(vis_hbm.at[pl.ds(pl.multiple_of(g * share, 16), share)], vbuf, v_sem)
    v_copy.start()
    p_copy = pltpu.make_async_copy(proj_hbm, pbuf, p_sem)
    p_copy.start()
    n_copy = pltpu.make_async_copy(gain_hbm, gain_ref, n_sem)
    n_copy.start()

    dests, sources = [], []
    for k in range(units):
        row = g * share + k * unit
        to = row // cap
        at = dp * cap + row % cap
        dests.append((to, at // share, at % share // unit))
        src_dp = row // cap
        src_row = dp * cap + row % cap
        sources.append((src_dp, src_row // share))

    def is_me(d_index, g_index):
        return jnp.logical_and(d_index == dp, g_index == g)

    barrier = pltpu.get_barrier_semaphore()
    pl.semaphore_signal(barrier, inc=1, device_id=(dp, t, other), device_id_type=MESH)
    for m in range(1, n_t):
        pl.semaphore_signal(barrier, inc=1, device_id=(dp, xor(t, m, bits), s), device_id_type=MESH)
    expect = jnp.int32(n_t)
    for k in range(units):
        src_dp, src_g = sources[k]

        @pl.when(jnp.logical_not(is_me(src_dp, src_g)))
        def _():
            pl.semaphore_signal(barrier, inc=1, device_id=(src_dp, src_g // 2, src_g % 2), device_id_type=MESH)

        expect = expect + jnp.where(is_me(dests[k][0], dests[k][1]), 0, 1)

    img_rows = rows // slots
    per = slots // samples
    live, owner = [], []
    for j in range(slots):
        live.append(jnp.where(j % per < cnt_ref[j // per], til_ref[j % per, j // per] * TILE_TOK, 0))
        owner.append(own_ref[j % per, j // per])
    lane = lax.broadcasted_iota(jnp.int32, (1, rows), 1)
    slot, tok = lane // img_rows, lane % img_rows
    target = jnp.full((1, rows), -1, jnp.int32)
    for j in range(slots):
        base = owner[j] * cap
        for i in range(j):
            base = base + jnp.where(owner[i] == owner[j], live[i], 0)
        target = jnp.where(slot == j, jnp.where(tok < live[j], base + tok, -1), target)
    placing = (lax.broadcasted_iota(jnp.int32, (placed, rows), 0) == target).astype(F32).astype(BF16)

    g_copy.wait()
    left = jnp.concatenate([grad_ref[:, 0, :], grad_ref[:, 1, :]], axis=1)
    if early:
        left = jnp.dot(placing, left, preferred_element_type=F32).astype(BF16)

    def multiply(q, sibling):
        i, cp = w_copies[q, sibling]
        cp.wait()
        return jnp.dot(left, wbuf[i], preferred_element_type=F32)

    def sib_copy(q):
        return pltpu.make_async_remote_copy(
            sib_out.at[q], sib_in.at[q], sib_s.at[q], sib_r.at[q], device_id=(dp, t, other), device_id_type=MESH
        )

    def half_copy(q):
        to = flip(t, stage_of(q, bits), s)
        return pltpu.make_async_remote_copy(
            half_out.at[q], half_in.at[q], half_s.at[q], half_r.at[q], device_id=(dp, to, s), device_id_type=MESH
        )

    first = True
    for q, sibling in order:
        if sibling:
            sib_out[q] = multiply(q, True).astype(BF16)
            if first:
                pl.semaphore_wait(barrier, expect)
                first = False
            sib_copy(q).start()
        else:
            value = multiply(q, False)
            sib_copy(q).wait_recv()
            value = value + sib_in[q].astype(F32)
            if q > 0 and stage_of(q, bits) == 0:
                half_out[q] = value.astype(BF16)
                half_copy(q).start()
            else:
                local[q] = value

    v_copy.wait()
    n_copy.wait()
    gain = gain_ref[...].reshape(1, gain_ref.shape[0])
    states = vbuf[...].astype(F32)
    centre = states - jnp.mean(states, axis=1, keepdims=True)
    inverse = lax.rsqrt(jnp.mean(centre * centre, axis=1, keepdims=True) + 1e-05)
    normed = centre * inverse

    for q in reversed(range(n_t // 2)):
        value = local[q]
        for step in range(stage_of(q, bits)):
            sent = q + (n_t >> (step + 1))
            half_copy(sent).wait_recv()
            value = value + half_in[sent].astype(F32)
        if q > 0:
            half_out[q] = value.astype(BF16)
            half_copy(q).start()
    features = value.astype(BF16)
    if not early:
        features = jnp.dot(placing, features, preferred_element_type=F32).astype(BF16)
    p_copy.wait()
    product = jnp.dot(features, pbuf[...], preferred_element_type=F32).astype(BF16)
    for i in range(groups):
        term[i % 2, i // 2] = product[i * share:(i + 1) * share]

    pair = pltpu.make_async_remote_copy(
        term.at[other], pair_in, pair_s, pair_r, device_id=(dp, t, other), device_id_type=MESH
    )
    pair.start()
    pair.wait_recv()

    def chip_copy(m):
        return pltpu.make_async_remote_copy(
            pair_out.at[m], chip_in.at[m], chip_s.at[m], chip_r.at[m],
            device_id=(dp, xor(t, m, bits), s), device_id_type=MESH,
        )

    for m in range(1, n_t):
        to = xor(t, m, bits)
        pair_out[m] = (term[s, to].astype(F32) + pair_in[to].astype(F32)).astype(BF16)
        chip_copy(m).start()
    total = term[s, t].astype(F32) + pair_in[t].astype(F32)
    for m in range(1, n_t):
        chip_copy(m).wait_recv()
        total = total + chip_in[m].astype(F32)
    for k in range(units):
        done[k] = total[k * unit:(k + 1) * unit].astype(done.dtype)

    def unit_copy(k):
        to, to_g, at = dests[k]
        return pltpu.make_async_remote_copy(
            done.at[k], unit_in.at[at], unit_s.at[k], unit_r.at[at],
            device_id=(to, to_g // 2, to_g % 2), device_id_type=MESH,
        )

    for k in range(units):
        mine = is_me(dests[k][0], dests[k][1])

        @pl.when(mine)
        def _():
            unit_in[dests[k][2]] = done[k]

        @pl.when(jnp.logical_not(mine))
        def _():
            unit_copy(k).start()

    for k in range(units):

        @pl.when(jnp.logical_not(is_me(*sources[k])))
        def _():
            pltpu.make_async_remote_copy(
                done.at[k], unit_in.at[k], unit_s.at[k], unit_r.at[k],
                device_id=(sources[k][0], sources[k][1] // 2, sources[k][1] % 2), device_id_type=MESH,
            ).wait_recv()

    norm_grad = jnp.concatenate([unit_in[k] for k in range(units)], axis=0).astype(F32)
    scaled = norm_grad * gain
    out_ref[...] = (
        scaled
        - jnp.mean(scaled, axis=1, keepdims=True)
        - normed * jnp.mean(scaled * normed, axis=1, keepdims=True)
    ) * inverse

    for q in range(n_t):
        sib_copy(q).wait_send()
    for q in range(1, n_t):
        half_copy(q).wait_send()
    pair.wait_send()
    for m in range(1, n_t):
        chip_copy(m).wait_send()
    for k in range(units):

        @pl.when(jnp.logical_not(is_me(dests[k][0], dests[k][1])))
        def _():
            unit_copy(k).wait_send()


def solution(mesh):
    n_dp, n_t = mesh.shape["dp"], mesh.shape["tensor"]
    bits = n_t.bit_length() - 1

    def per_device(grad_kv, kv_weight, image_count, tile_count, image_owner, proj_weight, vision_states, norm_gain):
        rows, width = grad_kv.shape[0], proj_weight.shape[1]
        depth = 2 * grad_kv.shape[3]
        samples = image_owner.shape[0]
        slots = samples * image_owner.shape[1]
        cap = rows // slots * max(1, slots // n_dp)
        placed = n_dp * cap
        share = placed // (2 * n_t)
        unit = min(cap, share)
        units = share // unit
        dm = kv_weight.shape[3]
        col = dm // (2 * n_t)
        mid = rows
        sizes = (n_dp, n_t, bits, rows, cap, placed, share, unit, samples, slots)
        moved = BF16 if unit % 16 == 0 else F32
        vmem, smem, hbm = (pl.BlockSpec(memory_space=m) for m in (pltpu.VMEM, pltpu.SMEM, pltpu.HBM))
        dma = pltpu.SemaphoreType.DMA
        return pl.pallas_call(
            functools.partial(kernel, sizes),
            out_shape=jax.ShapeDtypeStruct((share, width), F32),
            in_specs=[smem, smem, smem, hbm, hbm, hbm, hbm, hbm],
            out_specs=vmem,
            scratch_shapes=[
                pltpu.VMEM((rows, 2, grad_kv.shape[3]), BF16),
                pltpu.VMEM((width,), F32),
                pltpu.VMEM((2 * n_t, depth, col), BF16),
                pltpu.VMEM((col, width), BF16),
                pltpu.VMEM((share, width), BF16),
                pltpu.VMEM((n_t, mid, col), BF16),
                pltpu.VMEM((n_t, mid, col), BF16),
                pltpu.VMEM((max(1, n_t // 2), mid, col), F32),
                pltpu.VMEM((n_t, mid, col), BF16),
                pltpu.VMEM((n_t, mid, col), BF16),
                pltpu.VMEM((2, n_t, share, width), BF16),
                pltpu.VMEM((n_t, share, width), BF16),
                pltpu.VMEM((n_t, share, width), BF16),
                pltpu.VMEM((n_t, share, width), BF16),
                pltpu.VMEM((units, unit, width), moved),
                pltpu.VMEM((units, unit, width), moved),
                dma, dma, dma((2 * n_t,)), dma, dma,
                dma((n_t,)), dma((n_t,)), dma((n_t,)), dma((n_t,)), dma, dma,
                dma((n_t,)), dma((n_t,)), dma((units,)), dma((units,)),
            ],
            compiler_params=pltpu.CompilerParams(
                collective_id=0, has_side_effects=True, vmem_limit_bytes=56 * 1024 * 1024
            ),
        )(
            image_count, tile_count.T, image_owner.T, grad_kv.reshape(rows, 2, grad_kv.shape[3]),
            kv_weight.reshape(depth, dm), proj_weight, vision_states, norm_gain,
        )

    return jax.shard_map(
        per_device,
        mesh=mesh,
        in_specs=(
            P("dp", "section", None, "tensor"),
            P("section", None, "tensor", None),
            P("dp"),
            P("dp", None),
            P("dp", None),
            P(("tensor", "section"), None),
            P("dp", None),
            P(),
        ),
        out_specs=P(("dp", "tensor", "section"), None),
        check_vma=False,
    )
```

```python
import functools
import jax
import jax.numpy as jnp
from jax import lax
from jax.experimental import pallas as pl
from jax.experimental.pallas import tpu as pltpu
from jax.sharding import PartitionSpec as P

TILE_TOK = 2
PIECES = 2
BANDS = 2
MESH = pl.DeviceIdType.MESH
F32 = jnp.float32
BF16 = jnp.bfloat16


def stage_of(q, bits):
    return bits - q.bit_length()


def block_mask(q, core, bits):
    mask = 0
    for step in range(bits):
        if q >> (bits - 1 - step) & 1:
            mask = mask + lax.shift_left(jnp.int32(1), jnp.int32((step + core) % bits))
    return mask


def xor(a, b, bits):
    total = 0
    for bit in range(bits):
        x, y = a // (1 << bit) % 2, b // (1 << bit) % 2
        total = total + (x + y - 2 * x * y) * (1 << bit)
    return total


def kernel(
    sizes, cnt_ref, til_ref, own_ref, grad_hbm, w_hbm, proj_hbm, vis_hbm, gain_hbm, out_ref,
    grad_ref, gain_ref,    wbuf, pbuf, vbuf, sib_out, sib_in, local, half_out, half_in, term, pair_in, pair_out, chip_in,
    done, unit_in,
    g_sem, n_sem, w_sem, p_sem, v_sem, sib_s, sib_r, half_s, half_r, pair_s, pair_r, chip_s, chip_r, unit_s, unit_r,
):
    n_dp, n_t, bits, rows, cap, placed, share, unit, samples, slots = sizes
    groups = 2 * n_t
    dp, t, s = lax.axis_index("dp"), lax.axis_index("tensor"), lax.axis_index("section")
    g = t * 2 + s
    other = 1 - s
    piece = wbuf.shape[2]
    wide = term.shape[4]
    units = share // unit
    early = placed <= rows

    def flip(t_index, step, core):
        bit = 1
        if bits > 1:
            shift = (step + core) % bits
            bit = sum(jnp.where(shift == i, 1 << i, 0) for i in range(bits))
        digit = t_index // bit % 2
        return t_index + (1 - 2 * digit) * bit

    def tensor_of(q, core):
        index = t
        for step in range(bits):
            if q >> (bits - 1 - step) & 1:
                index = flip(index, step, core)
        return index

    pieces = [(q, c) for q in reversed(range(n_t)) for c in range(PIECES)]
    order = [(pieces[0], True)]
    for i, here in enumerate(pieces[1:]):
        order += [(here, True), (pieces[i], False)]
    order += [(pieces[-1], False)]
    g_copy = pltpu.make_async_copy(grad_hbm, grad_ref, g_sem)
    g_copy.start()
    w_copies = {}
    for i, ((q, c), sibling) in enumerate(order):
        core = other if sibling else s
        block = tensor_of(q, core) * 2 + core
        cp = pltpu.make_async_copy(
            w_hbm.at[:, pl.ds(pl.multiple_of((block * PIECES + c) * piece, 128), piece)], wbuf.at[i], w_sem.at[i]
        )
        cp.start()
        w_copies[(q, c), sibling] = (i, cp)
    v_copy = pltpu.make_async_copy(vis_hbm.at[pl.ds(pl.multiple_of(g * share, 16), share)], vbuf, v_sem)
    v_copy.start()
    p_copy = pltpu.make_async_copy(proj_hbm, pbuf, p_sem)
    p_copy.start()
    n_copy = pltpu.make_async_copy(gain_hbm, gain_ref, n_sem)
    n_copy.start()

    dests, sources = [], []
    for k in range(units):
        row = g * share + k * unit
        to = row // cap
        at = dp * cap + row % cap
        dests.append((to, at // share, at % share // unit))
        src_dp = row // cap
        src_row = dp * cap + row % cap
        sources.append((src_dp, src_row // share))

    def is_me(d_index, g_index):
        return jnp.logical_and(d_index == dp, g_index == g)

    barrier = pltpu.get_barrier_semaphore()
    pl.semaphore_signal(barrier, inc=1, device_id=(dp, t, other), device_id_type=MESH)
    for m in range(1, n_t):
        pl.semaphore_signal(barrier, inc=1, device_id=(dp, xor(t, m, bits), s), device_id_type=MESH)
    expect = jnp.int32(n_t)
    for k in range(units):
        src_dp, src_g = sources[k]

        @pl.when(jnp.logical_not(is_me(src_dp, src_g)))
        def _():
            pl.semaphore_signal(barrier, inc=1, device_id=(src_dp, src_g // 2, src_g % 2), device_id_type=MESH)

        expect = expect + jnp.where(is_me(dests[k][0], dests[k][1]), 0, 1)

    img_rows = rows // slots
    per = slots // samples
    live, owner = [], []
    for j in range(slots):
        live.append(jnp.where(j % per < cnt_ref[j // per], til_ref[j % per, j // per] * TILE_TOK, 0))
        owner.append(own_ref[j % per, j // per])
    lane = lax.broadcasted_iota(jnp.int32, (1, rows), 1)
    slot, tok = lane // img_rows, lane % img_rows
    target = jnp.full((1, rows), -1, jnp.int32)
    for j in range(slots):
        base = owner[j] * cap
        for i in range(j):
            base = base + jnp.where(owner[i] == owner[j], live[i], 0)
        target = jnp.where(slot == j, jnp.where(tok < live[j], base + tok, -1), target)
    placing = (lax.broadcasted_iota(jnp.int32, (placed, rows), 0) == target).astype(F32).astype(BF16)

    g_copy.wait()
    left = jnp.concatenate([grad_ref[:, 0, :], grad_ref[:, 1, :]], axis=1)
    if early:
        left = jnp.dot(placing, left, preferred_element_type=F32).astype(BF16)

    def multiply(here, sibling):
        i, cp = w_copies[here, sibling]
        cp.wait()
        return jnp.dot(left, wbuf[i], preferred_element_type=F32)

    def sib_copy(here):
        at = here[0] * PIECES + here[1]
        return pltpu.make_async_remote_copy(
            sib_out.at[at], sib_in.at[at], sib_s.at[at], sib_r.at[at], device_id=(dp, t, other), device_id_type=MESH
        )

    def half_copy(here):
        at = here[0] * PIECES + here[1]
        to = flip(t, stage_of(here[0], bits), s)
        return pltpu.make_async_remote_copy(
            half_out.at[at], half_in.at[at], half_s.at[at], half_r.at[at], device_id=(dp, to, s), device_id_type=MESH
        )

    def gathered(here, value):
        q, c = here
        for step in range(stage_of(q, bits)):
            sent = q + (n_t >> (step + 1))
            half_copy((sent, c)).wait_recv()
            value = value + half_in[sent * PIECES + c].astype(F32)
        return value

    def send_half(here, value):
        half_out[here[0] * PIECES + here[1]] = value.astype(BF16)
        half_copy(here).start()

    waiting = []
    for count, (here, sibling) in enumerate(order):
        q, c = here
        if sibling:
            sib_out[q * PIECES + c] = multiply(here, True).astype(BF16)
            if count == 0:
                pl.semaphore_wait(barrier, expect)
            sib_copy(here).start()
            continue
        if q == 0 and c == PIECES - 2:
            for q_held, c_held in waiting:
                send_half((q_held, c_held), gathered((q_held, c_held), local[q_held * PIECES + c_held]))
            waiting = []
        value = multiply(here, False)
        sib_copy(here).wait_recv()
        value = value + sib_in[q * PIECES + c].astype(F32)
        if q > 0 and stage_of(q, bits) == 0:
            send_half(here, value)
        else:
            local[q * PIECES + c] = value
            if q > 0:
                waiting.append(here)

    v_copy.wait()
    n_copy.wait()
    gain = gain_ref[...].reshape(1, gain_ref.shape[0])
    states = vbuf[...].astype(F32)
    centre = states - jnp.mean(states, axis=1, keepdims=True)
    inverse = lax.rsqrt(jnp.mean(centre * centre, axis=1, keepdims=True) + 1e-05)
    normed = centre * inverse

    features = jnp.concatenate(
        [gathered((0, c), local[c]).astype(BF16) for c in range(PIECES)], axis=1
    )
    if not early:
        features = jnp.dot(placing, features, preferred_element_type=F32).astype(BF16)
    p_copy.wait()

    def pair_copy(b):
        return pltpu.make_async_remote_copy(
            term.at[b, other], pair_in.at[b], pair_s.at[b], pair_r.at[b],
            device_id=(dp, t, other), device_id_type=MESH,
        )

    def chip_copy(b, m):
        at = b * n_t + m
        return pltpu.make_async_remote_copy(
            pair_out.at[at], chip_in.at[at], chip_s.at[at], chip_r.at[at],
            device_id=(dp, xor(t, m, bits), s), device_id_type=MESH,
        )

    def unit_copy(b, k):
        to, to_g, at = dests[k]
        return pltpu.make_async_remote_copy(
            done.at[b * units + k], unit_in.at[b * units + at], unit_s.at[b * units + k], unit_r.at[b * units + at],
            device_id=(to, to_g // 2, to_g % 2), device_id_type=MESH,
        )

    for b in range(BANDS):
        product = jnp.dot(features, pbuf[:, b * wide:(b + 1) * wide], preferred_element_type=F32).astype(BF16)
        for i in range(groups):
            term[b, i % 2, i // 2] = product[i * share:(i + 1) * share]
        pair_copy(b).start()
    for b in range(BANDS):
        pair_copy(b).wait_recv()
        for m in range(1, n_t):
            to = xor(t, m, bits)
            pair_out[b * n_t + m] = (term[b, s, to].astype(F32) + pair_in[b, to].astype(F32)).astype(BF16)
            chip_copy(b, m).start()
    for b in range(BANDS):
        total = term[b, s, t].astype(F32) + pair_in[b, t].astype(F32)
        for m in range(1, n_t):
            chip_copy(b, m).wait_recv()
            total = total + chip_in[b * n_t + m].astype(F32)
        for k in range(units):
            done[b * units + k] = total[k * unit:(k + 1) * unit].astype(done.dtype)
            mine = is_me(dests[k][0], dests[k][1])

            @pl.when(mine)
            def _():
                unit_in[b * units + dests[k][2]] = done[b * units + k]

            @pl.when(jnp.logical_not(mine))
            def _():
                unit_copy(b, k).start()

    for b in range(BANDS):
        for k in range(units):

            @pl.when(jnp.logical_not(is_me(*sources[k])))
            def _():
                at = b * units + k
                pltpu.make_async_remote_copy(
                    done.at[at], unit_in.at[at], unit_s.at[at], unit_r.at[at],
                    device_id=(sources[k][0], sources[k][1] // 2, sources[k][1] % 2), device_id_type=MESH,
                ).wait_recv()

    norm_grad = jnp.concatenate(
        [jnp.concatenate([unit_in[b * units + k] for k in range(units)], axis=0) for b in range(BANDS)], axis=1
    ).astype(F32)
    scaled = norm_grad * gain
    out_ref[...] = (
        scaled
        - jnp.mean(scaled, axis=1, keepdims=True)
        - normed * jnp.mean(scaled * normed, axis=1, keepdims=True)
    ) * inverse

    for here in pieces:
        sib_copy(here).wait_send()
        if here[0] > 0:
            half_copy(here).wait_send()
    for b in range(BANDS):
        pair_copy(b).wait_send()
        for m in range(1, n_t):
            chip_copy(b, m).wait_send()
        for k in range(units):

            @pl.when(jnp.logical_not(is_me(dests[k][0], dests[k][1])))
            def _():
                unit_copy(b, k).wait_send()


def solution(mesh):
    n_dp, n_t = mesh.shape["dp"], mesh.shape["tensor"]
    bits = n_t.bit_length() - 1

    def per_device(grad_kv, kv_weight, image_count, tile_count, image_owner, proj_weight, vision_states, norm_gain):
        rows, width = grad_kv.shape[0], proj_weight.shape[1]
        depth = 2 * grad_kv.shape[3]
        samples = image_owner.shape[0]
        slots = samples * image_owner.shape[1]
        cap = rows // slots * max(1, slots // n_dp)
        placed = n_dp * cap
        share = placed // (2 * n_t)
        unit = min(cap, share)
        units = share // unit
        dm = kv_weight.shape[3]
        col = dm // (2 * n_t)
        piece = col // PIECES
        wide = width // BANDS
        sizes = (n_dp, n_t, bits, rows, cap, placed, share, unit, samples, slots)
        moved = BF16 if unit % 16 == 0 else F32
        vmem, smem, hbm = (pl.BlockSpec(memory_space=m) for m in (pltpu.VMEM, pltpu.SMEM, pltpu.HBM))
        dma = pltpu.SemaphoreType.DMA
        return pl.pallas_call(
            functools.partial(kernel, sizes),
            out_shape=jax.ShapeDtypeStruct((share, width), F32),
            in_specs=[smem, smem, smem, hbm, hbm, hbm, hbm, hbm],
            out_specs=vmem,
            scratch_shapes=[
                pltpu.VMEM((rows, 2, grad_kv.shape[3]), BF16),
                pltpu.VMEM((width,), F32),
                pltpu.VMEM((2 * n_t * PIECES, depth, piece), BF16),
                pltpu.VMEM((col, width), BF16),
                pltpu.VMEM((share, width), BF16),
                pltpu.VMEM((n_t * PIECES, rows, piece), BF16),
                pltpu.VMEM((n_t * PIECES, rows, piece), BF16),
                pltpu.VMEM((n_t * PIECES // 2, rows, piece), F32),
                pltpu.VMEM((n_t * PIECES, rows, piece), BF16),
                pltpu.VMEM((n_t * PIECES, rows, piece), BF16),
                pltpu.VMEM((BANDS, 2, n_t, share, wide), BF16),
                pltpu.VMEM((BANDS, n_t, share, wide), BF16),
                pltpu.VMEM((BANDS * n_t, share, wide), BF16),
                pltpu.VMEM((BANDS * n_t, share, wide), BF16),
                pltpu.VMEM((BANDS * units, unit, wide), moved),
                pltpu.VMEM((BANDS * units, unit, wide), moved),
                dma, dma, dma((2 * n_t * PIECES,)), dma, dma,
                dma((n_t * PIECES,)), dma((n_t * PIECES,)), dma((n_t * PIECES,)), dma((n_t * PIECES,)),
                dma((BANDS,)), dma((BANDS,)), dma((BANDS * n_t,)), dma((BANDS * n_t,)),
                dma((BANDS * units,)), dma((BANDS * units,)),
            ],
            compiler_params=pltpu.CompilerParams(
                collective_id=0, has_side_effects=True, vmem_limit_bytes=56 * 1024 * 1024
            ),
        )(
            image_count, tile_count.T, image_owner.T, grad_kv.reshape(rows, 2, grad_kv.shape[3]),
            kv_weight.reshape(depth, dm), proj_weight, vision_states, norm_gain,
        )

    return jax.shard_map(
        per_device,
        mesh=mesh,
        in_specs=(
            P("dp", "section", None, "tensor"),
            P("section", None, "tensor", None),
            P("dp"),
            P("dp", None),
            P("dp", None),
            P(("tensor", "section"), None),
            P("dp", None),
            P(),
        ),
        out_specs=P(("dp", "tensor", "section"), None),
        check_vma=False,
    )
```

```python
import functools
import jax
import jax.numpy as jnp
from jax import lax
from jax.experimental import pallas as pl
from jax.experimental.pallas import tpu as pltpu
from jax.sharding import PartitionSpec as P

TILE_TOK = 2
PIECES = 1
BANDS = 2
MESH = pl.DeviceIdType.MESH
F32 = jnp.float32
BF16 = jnp.bfloat16


def stage_of(q, bits):
    return bits - q.bit_length()


def block_mask(q, core, bits):
    mask = 0
    for step in range(bits):
        if q >> (bits - 1 - step) & 1:
            mask = mask + lax.shift_left(jnp.int32(1), jnp.int32((step + core) % bits))
    return mask


def xor(a, b, bits):
    total = 0
    for bit in range(bits):
        x, y = a // (1 << bit) % 2, b // (1 << bit) % 2
        total = total + (x + y - 2 * x * y) * (1 << bit)
    return total


def kernel(
    sizes, cnt_ref, til_ref, own_ref, grad_hbm, w_hbm, proj_hbm, vis_hbm, gain_hbm, out_ref,
    grad_ref, gain_ref,    wbuf, pbuf, vbuf, sib_out, sib_in, local, half_out, half_in, term, pair_in, pair_out, chip_in,
    done, unit_in,
    g_sem, n_sem, w_sem, p_sem, v_sem, sib_s, sib_r, half_s, half_r, pair_s, pair_r, chip_s, chip_r, unit_s, unit_r,
):
    n_dp, n_t, bits, rows, cap, placed, share, unit, samples, slots = sizes
    groups = 2 * n_t
    dp, t, s = lax.axis_index("dp"), lax.axis_index("tensor"), lax.axis_index("section")
    g = t * 2 + s
    other = 1 - s
    piece = wbuf.shape[2]
    wide = term.shape[4]
    units = share // unit
    early = placed <= rows

    def flip(t_index, step, core):
        bit = 1
        if bits > 1:
            shift = (step + core) % bits
            bit = sum(jnp.where(shift == i, 1 << i, 0) for i in range(bits))
        digit = t_index // bit % 2
        return t_index + (1 - 2 * digit) * bit

    def tensor_of(q, core):
        index = t
        for step in range(bits):
            if q >> (bits - 1 - step) & 1:
                index = flip(index, step, core)
        return index

    pieces = [(q, c) for q in reversed(range(n_t)) for c in range(PIECES)]
    order = [(pieces[0], True)]
    for i, here in enumerate(pieces[1:]):
        order += [(here, True), (pieces[i], False)]
    order += [(pieces[-1], False)]
    g_copy = pltpu.make_async_copy(grad_hbm, grad_ref, g_sem)
    g_copy.start()
    w_copies = {}
    for i, ((q, c), sibling) in enumerate(order):
        core = other if sibling else s
        block = tensor_of(q, core) * 2 + core
        cp = pltpu.make_async_copy(
            w_hbm.at[:, pl.ds(pl.multiple_of((block * PIECES + c) * piece, 128), piece)], wbuf.at[i], w_sem.at[i]
        )
        cp.start()
        w_copies[(q, c), sibling] = (i, cp)
    v_copy = pltpu.make_async_copy(vis_hbm.at[pl.ds(pl.multiple_of(g * share, 16), share)], vbuf, v_sem)
    v_copy.start()
    p_copy = pltpu.make_async_copy(proj_hbm, pbuf, p_sem)
    p_copy.start()
    n_copy = pltpu.make_async_copy(gain_hbm, gain_ref, n_sem)
    n_copy.start()

    dests, sources = [], []
    for k in range(units):
        row = g * share + k * unit
        to = row // cap
        at = dp * cap + row % cap
        dests.append((to, at // share, at % share // unit))
        src_dp = row // cap
        src_row = dp * cap + row % cap
        sources.append((src_dp, src_row // share))

    def is_me(d_index, g_index):
        return jnp.logical_and(d_index == dp, g_index == g)

    barrier = pltpu.get_barrier_semaphore()
    pl.semaphore_signal(barrier, inc=1, device_id=(dp, t, other), device_id_type=MESH)
    for m in range(1, n_t):
        pl.semaphore_signal(barrier, inc=1, device_id=(dp, xor(t, m, bits), s), device_id_type=MESH)
    expect = jnp.int32(n_t)
    for k in range(units):
        src_dp, src_g = sources[k]

        @pl.when(jnp.logical_not(is_me(src_dp, src_g)))
        def _():
            pl.semaphore_signal(barrier, inc=1, device_id=(src_dp, src_g // 2, src_g % 2), device_id_type=MESH)

        expect = expect + jnp.where(is_me(dests[k][0], dests[k][1]), 0, 1)

    img_rows = rows // slots
    per = slots // samples
    live, owner = [], []
    for j in range(slots):
        live.append(jnp.where(j % per < cnt_ref[j // per], til_ref[j % per, j // per] * TILE_TOK, 0))
        owner.append(own_ref[j % per, j // per])
    lane = lax.broadcasted_iota(jnp.int32, (1, rows), 1)
    slot, tok = lane // img_rows, lane % img_rows
    target = jnp.full((1, rows), -1, jnp.int32)
    for j in range(slots):
        base = owner[j] * cap
        for i in range(j):
            base = base + jnp.where(owner[i] == owner[j], live[i], 0)
        target = jnp.where(slot == j, jnp.where(tok < live[j], base + tok, -1), target)
    placing = (lax.broadcasted_iota(jnp.int32, (placed, rows), 0) == target).astype(F32).astype(BF16)

    g_copy.wait()
    left = jnp.concatenate([grad_ref[:, 0, :], grad_ref[:, 1, :]], axis=1)
    if early:
        left = jnp.dot(placing, left, preferred_element_type=F32).astype(BF16)

    def multiply(here, sibling):
        i, cp = w_copies[here, sibling]
        cp.wait()
        return jnp.dot(left, wbuf[i], preferred_element_type=F32)

    def sib_copy(here):
        at = here[0] * PIECES + here[1]
        return pltpu.make_async_remote_copy(
            sib_out.at[at], sib_in.at[at], sib_s.at[at], sib_r.at[at], device_id=(dp, t, other), device_id_type=MESH
        )

    def half_copy(here):
        at = here[0] * PIECES + here[1]
        to = flip(t, stage_of(here[0], bits), s)
        return pltpu.make_async_remote_copy(
            half_out.at[at], half_in.at[at], half_s.at[at], half_r.at[at], device_id=(dp, to, s), device_id_type=MESH
        )

    def gathered(here, value):
        q, c = here
        for step in range(stage_of(q, bits)):
            sent = q + (n_t >> (step + 1))
            half_copy((sent, c)).wait_recv()
            value = value + half_in[sent * PIECES + c].astype(F32)
        return value

    def send_half(here, value):
        half_out[here[0] * PIECES + here[1]] = value.astype(BF16)
        half_copy(here).start()

    waiting = []
    for count, (here, sibling) in enumerate(order):
        q, c = here
        if sibling:
            sib_out[q * PIECES + c] = multiply(here, True).astype(BF16)
            if count == 0:
                pl.semaphore_wait(barrier, expect)
            sib_copy(here).start()
            continue
        if q == 0 and c == 0:
            for q_held, c_held in waiting:
                send_half((q_held, c_held), gathered((q_held, c_held), local[q_held * PIECES + c_held]))
            waiting = []
        value = multiply(here, False)
        sib_copy(here).wait_recv()
        value = value + sib_in[q * PIECES + c].astype(F32)
        if q > 0 and stage_of(q, bits) == 0:
            send_half(here, value)
        else:
            local[q * PIECES + c] = value
            if q > 0:
                waiting.append(here)

    v_copy.wait()
    n_copy.wait()
    gain = gain_ref[...].reshape(1, gain_ref.shape[0])
    states = vbuf[...].astype(F32)
    centre = states - jnp.mean(states, axis=1, keepdims=True)
    inverse = lax.rsqrt(jnp.mean(centre * centre, axis=1, keepdims=True) + 1e-05)
    normed = centre * inverse

    features = jnp.concatenate(
        [gathered((0, c), local[c]).astype(BF16) for c in range(PIECES)], axis=1
    )
    if not early:
        features = jnp.dot(placing, features, preferred_element_type=F32).astype(BF16)
    p_copy.wait()

    def pair_copy(b):
        return pltpu.make_async_remote_copy(
            term.at[b, other], pair_in.at[b], pair_s.at[b], pair_r.at[b],
            device_id=(dp, t, other), device_id_type=MESH,
        )

    def chip_copy(b, m):
        at = b * n_t + m
        return pltpu.make_async_remote_copy(
            pair_out.at[at], chip_in.at[at], chip_s.at[at], chip_r.at[at],
            device_id=(dp, xor(t, m, bits), s), device_id_type=MESH,
        )

    def unit_copy(b, k):
        to, to_g, at = dests[k]
        return pltpu.make_async_remote_copy(
            done.at[b * units + k], unit_in.at[b * units + at], unit_s.at[b * units + k], unit_r.at[b * units + at],
            device_id=(to, to_g // 2, to_g % 2), device_id_type=MESH,
        )

    for b in range(BANDS):
        product = jnp.dot(features, pbuf[:, b * wide:(b + 1) * wide], preferred_element_type=F32).astype(BF16)
        for i in range(groups):
            term[b, i % 2, i // 2] = product[i * share:(i + 1) * share]
        pair_copy(b).start()
    for b in range(BANDS):
        pair_copy(b).wait_recv()
        for m in range(1, n_t):
            to = xor(t, m, bits)
            pair_out[b * n_t + m] = (term[b, s, to].astype(F32) + pair_in[b, to].astype(F32)).astype(BF16)
            chip_copy(b, m).start()
    for b in range(BANDS):
        total = term[b, s, t].astype(F32) + pair_in[b, t].astype(F32)
        for m in range(1, n_t):
            chip_copy(b, m).wait_recv()
            total = total + chip_in[b * n_t + m].astype(F32)
        for k in range(units):
            done[b * units + k] = total[k * unit:(k + 1) * unit].astype(done.dtype)
            mine = is_me(dests[k][0], dests[k][1])

            @pl.when(mine)
            def _():
                unit_in[b * units + dests[k][2]] = done[b * units + k]

            @pl.when(jnp.logical_not(mine))
            def _():
                unit_copy(b, k).start()

    for b in range(BANDS):
        for k in range(units):

            @pl.when(jnp.logical_not(is_me(*sources[k])))
            def _():
                at = b * units + k
                pltpu.make_async_remote_copy(
                    done.at[at], unit_in.at[at], unit_s.at[at], unit_r.at[at],
                    device_id=(sources[k][0], sources[k][1] // 2, sources[k][1] % 2), device_id_type=MESH,
                ).wait_recv()

    norm_grad = jnp.concatenate(
        [jnp.concatenate([unit_in[b * units + k] for k in range(units)], axis=0) for b in range(BANDS)], axis=1
    ).astype(F32)
    scaled = norm_grad * gain
    out_ref[...] = (
        scaled
        - jnp.mean(scaled, axis=1, keepdims=True)
        - normed * jnp.mean(scaled * normed, axis=1, keepdims=True)
    ) * inverse

    for here in pieces:
        sib_copy(here).wait_send()
        if here[0] > 0:
            half_copy(here).wait_send()
    for b in range(BANDS):
        pair_copy(b).wait_send()
        for m in range(1, n_t):
            chip_copy(b, m).wait_send()
        for k in range(units):

            @pl.when(jnp.logical_not(is_me(dests[k][0], dests[k][1])))
            def _():
                unit_copy(b, k).wait_send()


def solution(mesh):
    n_dp, n_t = mesh.shape["dp"], mesh.shape["tensor"]
    bits = n_t.bit_length() - 1

    def per_device(grad_kv, kv_weight, image_count, tile_count, image_owner, proj_weight, vision_states, norm_gain):
        rows, width = grad_kv.shape[0], proj_weight.shape[1]
        depth = 2 * grad_kv.shape[3]
        samples = image_owner.shape[0]
        slots = samples * image_owner.shape[1]
        cap = rows // slots * max(1, slots // n_dp)
        placed = n_dp * cap
        share = placed // (2 * n_t)
        unit = min(cap, share)
        units = share // unit
        dm = kv_weight.shape[3]
        col = dm // (2 * n_t)
        piece = col // PIECES
        wide = width // BANDS
        sizes = (n_dp, n_t, bits, rows, cap, placed, share, unit, samples, slots)
        moved = BF16 if unit % 16 == 0 else F32
        vmem, smem, hbm = (pl.BlockSpec(memory_space=m) for m in (pltpu.VMEM, pltpu.SMEM, pltpu.HBM))
        dma = pltpu.SemaphoreType.DMA
        return pl.pallas_call(
            functools.partial(kernel, sizes),
            out_shape=jax.ShapeDtypeStruct((share, width), F32),
            in_specs=[smem, smem, smem, hbm, hbm, hbm, hbm, hbm],
            out_specs=vmem,
            scratch_shapes=[
                pltpu.VMEM((rows, 2, grad_kv.shape[3]), BF16),
                pltpu.VMEM((width,), F32),
                pltpu.VMEM((2 * n_t * PIECES, depth, piece), BF16),
                pltpu.VMEM((col, width), BF16),
                pltpu.VMEM((share, width), BF16),
                pltpu.VMEM((n_t * PIECES, rows, piece), BF16),
                pltpu.VMEM((n_t * PIECES, rows, piece), BF16),
                pltpu.VMEM((n_t * PIECES // 2, rows, piece), F32),
                pltpu.VMEM((n_t * PIECES, rows, piece), BF16),
                pltpu.VMEM((n_t * PIECES, rows, piece), BF16),
                pltpu.VMEM((BANDS, 2, n_t, share, wide), BF16),
                pltpu.VMEM((BANDS, n_t, share, wide), BF16),
                pltpu.VMEM((BANDS * n_t, share, wide), BF16),
                pltpu.VMEM((BANDS * n_t, share, wide), BF16),
                pltpu.VMEM((BANDS * units, unit, wide), moved),
                pltpu.VMEM((BANDS * units, unit, wide), moved),
                dma, dma, dma((2 * n_t * PIECES,)), dma, dma,
                dma((n_t * PIECES,)), dma((n_t * PIECES,)), dma((n_t * PIECES,)), dma((n_t * PIECES,)),
                dma((BANDS,)), dma((BANDS,)), dma((BANDS * n_t,)), dma((BANDS * n_t,)),
                dma((BANDS * units,)), dma((BANDS * units,)),
            ],
            compiler_params=pltpu.CompilerParams(
                collective_id=0, has_side_effects=True, vmem_limit_bytes=56 * 1024 * 1024
            ),
        )(
            image_count, tile_count.T, image_owner.T, grad_kv.reshape(rows, 2, grad_kv.shape[3]),
            kv_weight.reshape(depth, dm), proj_weight, vision_states, norm_gain,
        )

    return jax.shard_map(
        per_device,
        mesh=mesh,
        in_specs=(
            P("dp", "section", None, "tensor"),
            P("section", None, "tensor", None),
            P("dp"),
            P("dp", None),
            P("dp", None),
            P(("tensor", "section"), None),
            P("dp", None),
            P(),
        ),
        out_specs=P(("dp", "tensor", "section"), None),
        check_vma=False,
    )
```

```python
import functools
import jax
import jax.numpy as jnp
from jax import lax
from jax.experimental import pallas as pl
from jax.experimental.pallas import tpu as pltpu
from jax.sharding import PartitionSpec as P

TILE_TOK = 2
PIECES = 1
BANDS = 2
AHEAD = 3
MESH = pl.DeviceIdType.MESH
F32 = jnp.float32
BF16 = jnp.bfloat16


def stage_of(q, bits):
    return bits - q.bit_length()


def block_mask(q, core, bits):
    mask = 0
    for step in range(bits):
        if q >> (bits - 1 - step) & 1:
            mask = mask + lax.shift_left(jnp.int32(1), jnp.int32((step + core) % bits))
    return mask


def xor(a, b, bits):
    total = 0
    for bit in range(bits):
        x, y = a // (1 << bit) % 2, b // (1 << bit) % 2
        total = total + (x + y - 2 * x * y) * (1 << bit)
    return total


def kernel(
    sizes, cnt_ref, til_ref, own_ref, grad_hbm, w_hbm, proj_hbm, vis_hbm, gain_hbm, out_ref,
    grad_ref, gain_ref,    wbuf, pbuf, vbuf, sib_out, sib_in, local, half_out, half_in, term, pair_in, pair_out, chip_in,
    done, unit_in,
    g_sem, n_sem, w_sem, p_sem, v_sem, sib_s, sib_r, half_s, half_r, pair_s, pair_r, chip_s, chip_r, unit_s, unit_r,
):
    n_dp, n_t, bits, rows, cap, placed, share, unit, samples, slots = sizes
    groups = 2 * n_t
    dp, t, s = lax.axis_index("dp"), lax.axis_index("tensor"), lax.axis_index("section")
    g = t * 2 + s
    other = 1 - s
    piece = wbuf.shape[2]
    wide = term.shape[4]
    units = share // unit
    early = placed <= rows

    def flip(t_index, step, core):
        bit = 1
        if bits > 1:
            shift = (step + core) % bits
            bit = sum(jnp.where(shift == i, 1 << i, 0) for i in range(bits))
        digit = t_index // bit % 2
        return t_index + (1 - 2 * digit) * bit

    def tensor_of(q, core):
        index = t
        for step in range(bits):
            if q >> (bits - 1 - step) & 1:
                index = flip(index, step, core)
        return index

    pieces = [(q, c) for q in reversed(range(n_t)) for c in range(PIECES)]
    order = [(pieces[0], True)]
    for i, here in enumerate(pieces[1:]):
        order += [(here, True), (pieces[i], False)]
    order += [(pieces[-1], False)]
    g_copy = pltpu.make_async_copy(grad_hbm, grad_ref, g_sem)
    g_copy.start()
    w_copies = {}
    for i, ((q, c), sibling) in enumerate(order):
        core = other if sibling else s
        block = tensor_of(q, core) * 2 + core
        cp = pltpu.make_async_copy(
            w_hbm.at[:, pl.ds(pl.multiple_of((block * PIECES + c) * piece, 128), piece)], wbuf.at[i], w_sem.at[i]
        )
        if i < AHEAD:
            cp.start()
        w_copies[(q, c), sibling] = (i, cp)
    v_copy = pltpu.make_async_copy(vis_hbm.at[pl.ds(pl.multiple_of(g * share, 16), share)], vbuf, v_sem)
    v_copy.start()
    p_copy = pltpu.make_async_copy(proj_hbm, pbuf, p_sem)
    n_copy = pltpu.make_async_copy(gain_hbm, gain_ref, n_sem)
    n_copy.start()

    dests, sources = [], []
    for k in range(units):
        row = g * share + k * unit
        to = row // cap
        at = dp * cap + row % cap
        dests.append((to, at // share, at % share // unit))
        src_dp = row // cap
        src_row = dp * cap + row % cap
        sources.append((src_dp, src_row // share))

    def is_me(d_index, g_index):
        return jnp.logical_and(d_index == dp, g_index == g)

    barrier = pltpu.get_barrier_semaphore()
    pl.semaphore_signal(barrier, inc=1, device_id=(dp, t, other), device_id_type=MESH)
    for m in range(1, n_t):
        pl.semaphore_signal(barrier, inc=1, device_id=(dp, xor(t, m, bits), s), device_id_type=MESH)
    expect = jnp.int32(n_t)
    for k in range(units):
        src_dp, src_g = sources[k]

        @pl.when(jnp.logical_not(is_me(src_dp, src_g)))
        def _():
            pl.semaphore_signal(barrier, inc=1, device_id=(src_dp, src_g // 2, src_g % 2), device_id_type=MESH)

        expect = expect + jnp.where(is_me(dests[k][0], dests[k][1]), 0, 1)

    img_rows = rows // slots
    per = slots // samples
    live, owner = [], []
    for j in range(slots):
        live.append(jnp.where(j % per < cnt_ref[j // per], til_ref[j % per, j // per] * TILE_TOK, 0))
        owner.append(own_ref[j % per, j // per])
    lane = lax.broadcasted_iota(jnp.int32, (1, rows), 1)
    slot, tok = lane // img_rows, lane % img_rows
    target = jnp.full((1, rows), -1, jnp.int32)
    for j in range(slots):
        base = owner[j] * cap
        for i in range(j):
            base = base + jnp.where(owner[i] == owner[j], live[i], 0)
        target = jnp.where(slot == j, jnp.where(tok < live[j], base + tok, -1), target)
    placing = (lax.broadcasted_iota(jnp.int32, (placed, rows), 0) == target).astype(F32).astype(BF16)

    g_copy.wait()
    left = jnp.concatenate([grad_ref[:, 0, :], grad_ref[:, 1, :]], axis=1)
    if early:
        left = jnp.dot(placing, left, preferred_element_type=F32).astype(BF16)

    def multiply(here, sibling):
        i, cp = w_copies[here, sibling]
        cp.wait()
        if i + AHEAD < len(order):
            w_copies[order[i + AHEAD]][1].start()
        elif i + AHEAD == len(order):
            p_copy.start()
        return jnp.dot(left, wbuf[i], preferred_element_type=F32)

    def sib_copy(here):
        at = here[0] * PIECES + here[1]
        return pltpu.make_async_remote_copy(
            sib_out.at[at], sib_in.at[at], sib_s.at[at], sib_r.at[at], device_id=(dp, t, other), device_id_type=MESH
        )

    def half_copy(here):
        at = here[0] * PIECES + here[1]
        to = flip(t, stage_of(here[0], bits), s)
        return pltpu.make_async_remote_copy(
            half_out.at[at], half_in.at[at], half_s.at[at], half_r.at[at], device_id=(dp, to, s), device_id_type=MESH
        )

    def gathered(here, value):
        q, c = here
        for step in range(stage_of(q, bits)):
            sent = q + (n_t >> (step + 1))
            half_copy((sent, c)).wait_recv()
            value = value + half_in[sent * PIECES + c].astype(F32)
        return value

    def send_half(here, value):
        half_out[here[0] * PIECES + here[1]] = value.astype(BF16)
        half_copy(here).start()

    waiting = []
    for count, (here, sibling) in enumerate(order):
        q, c = here
        if sibling:
            sib_out[q * PIECES + c] = multiply(here, True).astype(BF16)
            if count == 0:
                pl.semaphore_wait(barrier, expect)
            sib_copy(here).start()
            continue
        if q == 0 and c == 0:
            for q_held, c_held in waiting:
                send_half((q_held, c_held), gathered((q_held, c_held), local[q_held * PIECES + c_held]))
            waiting = []
        value = multiply(here, False)
        sib_copy(here).wait_recv()
        value = value + sib_in[q * PIECES + c].astype(F32)
        if q > 0 and stage_of(q, bits) == 0:
            send_half(here, value)
        else:
            local[q * PIECES + c] = value
            if q > 0:
                waiting.append(here)

    v_copy.wait()
    n_copy.wait()
    gain = gain_ref[...].reshape(1, gain_ref.shape[0])
    states = vbuf[...].astype(F32)
    centre = states - jnp.mean(states, axis=1, keepdims=True)
    inverse = lax.rsqrt(jnp.mean(centre * centre, axis=1, keepdims=True) + 1e-05)
    normed = centre * inverse

    features = jnp.concatenate(
        [gathered((0, c), local[c]).astype(BF16) for c in range(PIECES)], axis=1
    )
    if not early:
        features = jnp.dot(placing, features, preferred_element_type=F32).astype(BF16)
    p_copy.wait()

    def pair_copy(b):
        return pltpu.make_async_remote_copy(
            term.at[b, other], pair_in.at[b], pair_s.at[b], pair_r.at[b],
            device_id=(dp, t, other), device_id_type=MESH,
        )

    def chip_copy(b, m):
        at = b * n_t + m
        return pltpu.make_async_remote_copy(
            pair_out.at[at], chip_in.at[at], chip_s.at[at], chip_r.at[at],
            device_id=(dp, xor(t, m, bits), s), device_id_type=MESH,
        )

    def unit_copy(b, k):
        to, to_g, at = dests[k]
        return pltpu.make_async_remote_copy(
            done.at[b * units + k], unit_in.at[b * units + at], unit_s.at[b * units + k], unit_r.at[b * units + at],
            device_id=(to, to_g // 2, to_g % 2), device_id_type=MESH,
        )

    for b in range(BANDS):
        product = jnp.dot(features, pbuf[:, b * wide:(b + 1) * wide], preferred_element_type=F32).astype(BF16)
        for i in range(groups):
            term[b, i % 2, i // 2] = product[i * share:(i + 1) * share]
        pair_copy(b).start()
    for b in range(BANDS):
        pair_copy(b).wait_recv()
        for m in range(1, n_t):
            to = xor(t, m, bits)
            pair_out[b * n_t + m] = (term[b, s, to].astype(F32) + pair_in[b, to].astype(F32)).astype(BF16)
            chip_copy(b, m).start()
    for b in range(BANDS):
        total = term[b, s, t].astype(F32) + pair_in[b, t].astype(F32)
        for m in range(1, n_t):
            chip_copy(b, m).wait_recv()
            total = total + chip_in[b * n_t + m].astype(F32)
        for k in range(units):
            done[b * units + k] = total[k * unit:(k + 1) * unit].astype(done.dtype)
            mine = is_me(dests[k][0], dests[k][1])

            @pl.when(mine)
            def _():
                unit_in[b * units + dests[k][2]] = done[b * units + k]

            @pl.when(jnp.logical_not(mine))
            def _():
                unit_copy(b, k).start()

    for b in range(BANDS):
        for k in range(units):

            @pl.when(jnp.logical_not(is_me(*sources[k])))
            def _():
                at = b * units + k
                pltpu.make_async_remote_copy(
                    done.at[at], unit_in.at[at], unit_s.at[at], unit_r.at[at],
                    device_id=(sources[k][0], sources[k][1] // 2, sources[k][1] % 2), device_id_type=MESH,
                ).wait_recv()

    norm_grad = jnp.concatenate(
        [jnp.concatenate([unit_in[b * units + k] for k in range(units)], axis=0) for b in range(BANDS)], axis=1
    ).astype(F32)
    scaled = norm_grad * gain
    out_ref[...] = (
        scaled
        - jnp.mean(scaled, axis=1, keepdims=True)
        - normed * jnp.mean(scaled * normed, axis=1, keepdims=True)
    ) * inverse

    for here in pieces:
        sib_copy(here).wait_send()
        if here[0] > 0:
            half_copy(here).wait_send()
    for b in range(BANDS):
        pair_copy(b).wait_send()
        for m in range(1, n_t):
            chip_copy(b, m).wait_send()
        for k in range(units):

            @pl.when(jnp.logical_not(is_me(dests[k][0], dests[k][1])))
            def _():
                unit_copy(b, k).wait_send()


def solution(mesh):
    n_dp, n_t = mesh.shape["dp"], mesh.shape["tensor"]
    bits = n_t.bit_length() - 1

    def per_device(grad_kv, kv_weight, image_count, tile_count, image_owner, proj_weight, vision_states, norm_gain):
        rows, width = grad_kv.shape[0], proj_weight.shape[1]
        depth = 2 * grad_kv.shape[3]
        samples = image_owner.shape[0]
        slots = samples * image_owner.shape[1]
        cap = rows // slots * max(1, slots // n_dp)
        placed = n_dp * cap
        share = placed // (2 * n_t)
        unit = min(cap, share)
        units = share // unit
        dm = kv_weight.shape[3]
        col = dm // (2 * n_t)
        piece = col // PIECES
        wide = width // BANDS
        sizes = (n_dp, n_t, bits, rows, cap, placed, share, unit, samples, slots)
        moved = BF16 if unit % 16 == 0 else F32
        vmem, smem, hbm = (pl.BlockSpec(memory_space=m) for m in (pltpu.VMEM, pltpu.SMEM, pltpu.HBM))
        dma = pltpu.SemaphoreType.DMA
        return pl.pallas_call(
            functools.partial(kernel, sizes),
            out_shape=jax.ShapeDtypeStruct((share, width), F32),
            in_specs=[smem, smem, smem, hbm, hbm, hbm, hbm, hbm],
            out_specs=vmem,
            scratch_shapes=[
                pltpu.VMEM((rows, 2, grad_kv.shape[3]), BF16),
                pltpu.VMEM((width,), F32),
                pltpu.VMEM((2 * n_t * PIECES, depth, piece), BF16),
                pltpu.VMEM((col, width), BF16),
                pltpu.VMEM((share, width), BF16),
                pltpu.VMEM((n_t * PIECES, rows, piece), BF16),
                pltpu.VMEM((n_t * PIECES, rows, piece), BF16),
                pltpu.VMEM((n_t * PIECES // 2, rows, piece), F32),
                pltpu.VMEM((n_t * PIECES, rows, piece), BF16),
                pltpu.VMEM((n_t * PIECES, rows, piece), BF16),
                pltpu.VMEM((BANDS, 2, n_t, share, wide), BF16),
                pltpu.VMEM((BANDS, n_t, share, wide), BF16),
                pltpu.VMEM((BANDS * n_t, share, wide), BF16),
                pltpu.VMEM((BANDS * n_t, share, wide), BF16),
                pltpu.VMEM((BANDS * units, unit, wide), moved),
                pltpu.VMEM((BANDS * units, unit, wide), moved),
                dma, dma, dma((2 * n_t * PIECES,)), dma, dma,
                dma((n_t * PIECES,)), dma((n_t * PIECES,)), dma((n_t * PIECES,)), dma((n_t * PIECES,)),
                dma((BANDS,)), dma((BANDS,)), dma((BANDS * n_t,)), dma((BANDS * n_t,)),
                dma((BANDS * units,)), dma((BANDS * units,)),
            ],
            compiler_params=pltpu.CompilerParams(
                collective_id=0, has_side_effects=True, vmem_limit_bytes=56 * 1024 * 1024
            ),
        )(
            image_count, tile_count.T, image_owner.T, grad_kv.reshape(rows, 2, grad_kv.shape[3]),
            kv_weight.reshape(depth, dm), proj_weight, vision_states, norm_gain,
        )

    return jax.shard_map(
        per_device,
        mesh=mesh,
        in_specs=(
            P("dp", "section", None, "tensor"),
            P("section", None, "tensor", None),
            P("dp"),
            P("dp", None),
            P("dp", None),
            P(("tensor", "section"), None),
            P("dp", None),
            P(),
        ),
        out_specs=P(("dp", "tensor", "section"), None),
        check_vma=False,
    )
```
